256 devices in a mesh: dp: 4 (over z_lo), fsdp: 64 (over z_hi, y, x, core).
Axes of the slice: x: 4, y: 4, z: 8 (z_hi: 2, z_lo: 4; z = z_hi * 4 + z_lo), core: 2. Of those that a mesh axis runs over, the one named last changes fastest.
Arguments:
- grads: bfloat16 [4, 256, 2048, 256], P('dp', None, 'fsdp'), may hold values from -6 to 6
- owner: int32 [256], replicated, may hold values from 0 to 63, as said below
Outputs:
- owned: bfloat16 [4, 64, 2, 2048, 256], P('dp', 'fsdp')
The draws below stay inside these ranges and needn't reach their ends.
Inputs may be any that keep to these rules, and one draw needn't show every extreme that they name: In each block of 64 consecutive matrices no owner appears more than 2 times, and some owner appears exactly 2 times.
All inputs are finite; a program needn't handle non-finite values.
Results may differ from the reference program's by a relative error of at most 0.02.
Values may be sent and summed in bfloat16 or wider, within the bound.
A program may use at most 64 MiB of HBM per device.

```python
import math
import jax
import jax.numpy as jnp
from jax import lax

R = 2048
C = 256
CAP = 2
ITERS = 3
PER = 64
GROUPS = 4
OWNERS = 64
MATS = 256


def draw_owner(key, part):
    key = jax.random.fold_in(key, 7)
    lowest = max(1, PER - OWNERS)
    highest = PER // 2

    def single_block(block_key):
        first, second, third = jax.random.split(block_key, 3)
        ranking = jax.random.permutation(first, OWNERS)
        doubled = jax.random.randint(second, (), lowest, highest + 1)
        index = jnp.arange(PER, dtype=jnp.int32)
        picked = jnp.where(index < 2 * doubled, index // 2, index - doubled)
        owners_list = ranking[picked]
        order = jax.random.permutation(third, PER)
        return owners_list[order]
    blocks = jax.vmap(single_block)(jax.random.split(key, GROUPS))
    return blocks.reshape(-1).astype(jnp.int32)


def block_levels(rng, extent, cuts, smallest, top_value):
    def one(dim, shards_of):
        draws = jax.random.uniform(jax.random.fold_in(jax.random.fold_in(rng, 6), dim), (shards_of,), jnp.float32, smallest / len(cuts), top_value / len(cuts))
        return jnp.repeat(jnp.exp(draws), extent[dim] // shards_of).reshape((-1,) + (1,) * (len(extent) - dim - 1))

    factor_of = one(*cuts[0])
    for cut in cuts[1:]:
        factor_of = factor_of * one(*cut)
    return factor_of


def centred(own_key, shape, spread, most, shards=(), held_as=jnp.bfloat16):
    result = spread * jax.random.normal(own_key, shape, jnp.float32)
    if shards:
        result = result * block_levels(own_key, shape, shards, -0.22, 0.18)
    return jnp.clip(result, -most, most).astype(held_as)


def setup_inputs(seed: int = 0) -> dict:
    keys = jax.random.split(jax.random.key(seed), 3)
    grads = centred(keys[0], (GROUPS, MATS, R, C), 1.0, 6.0, ((0, 4), (2, 64)))
    owner = draw_owner(jax.random.fold_in(keys[2], 71), 0)
    return {"grads": grads, "owner": owner}


def newton(matrix, scale_out):
    values = matrix.astype(jnp.float32)
    norm = jnp.sqrt(jnp.sum(values * values))
    state = (values / (norm + 1e-07)).astype(jnp.bfloat16)
    for step in range(ITERS):
        gram = lax.dot_general(state, state, (((0,), (0,)), ((), ())), preferred_element_type=jnp.float32).astype(jnp.bfloat16)
        square = jnp.dot(gram, gram, preferred_element_type=jnp.float32)
        poly = (-4.775 * gram.astype(jnp.float32) + 2.0315 * square).astype(jnp.bfloat16)
        update = 3.4445 * state.astype(jnp.float32) + jnp.dot(state, poly, preferred_element_type=jnp.float32)
        if step + 1 < ITERS:
            state = update.astype(jnp.bfloat16)
        else:
            state = (update * scale_out).astype(jnp.bfloat16)
    return state

def reference(grads, owner):
    groups, matrices, rows, cols = grads.shape
    per_block = matrices // groups
    scale_out = 0.2 * math.sqrt(max(rows, cols))

    def single(index):
        stacked = lax.dynamic_index_in_dim(grads, index, 1, keepdims=False)
        summed = lax.optimization_barrier(jnp.sum(stacked.astype(jnp.float32), axis=0)).astype(jnp.bfloat16)
        return newton(summed, scale_out)
    results = lax.map(single, jnp.arange(matrices, dtype=jnp.int32))
    index = jnp.arange(matrices, dtype=jnp.int32)
    block_id = index // per_block
    earlier = (owner[:, None] == owner[None, :]) & (block_id[:, None] == block_id[None, :]) & (index[None, :] < index[:, None])
    slot = lax.optimization_barrier(jnp.sum(earlier.astype(jnp.int32), axis=1)).astype(jnp.int32)
    owned = jnp.zeros((groups, OWNERS, CAP, rows, cols), results.dtype)
    return owned.at[block_id, owner, slot].set(results)
```

```python
import functools
import math

import jax
import jax.numpy as jnp
from jax import lax
from jax.experimental import pallas as pl
from jax.experimental.pallas import tpu as pltpu
from jax.sharding import PartitionSpec as P

MESH = pl.DeviceIdType.MESH
CAP = 2
HALVES = 2
PLANE = 32
CHUNKS = 4
TR, TC = 16, 128
PER = 64
SURE = 24
FULL = PER - SURE
ORIGIN = ((1, 0), (1, 1), (0, 3), (0, 2), (0, 1))
BACK = ((1, 3), (1, 2), (0, 0))
LISTS = ORIGIN + BACK


def size(flow):
    return SURE if flow in ((1, 1), (1, 2)) else FULL


def exchange(tab_ref, grads_ref, out_ref, g0, g1, g2, g3, own, a, b, c, xf, xs, sf, dsp,
             g_sem, a_s, a_r, b_s, b_r, c_s, c_r, x_s, x_r, u_s, u_r, p_s, p_r):
    gv = (g0, g1, g2, g3)
    g = lax.axis_index("dp")
    f = lax.axis_index("fsdp")
    h, me = f // PLANE, f % PLANE
    z = h * 4 + g
    side = g // 2
    dirn = 1 - 2 * side
    outer = (g == 0) | (g == 3)
    inner = jnp.logical_not(outer)

    def along_z(step):
        zz = (z + step + 16) % 8
        return (zz % 4, (zz // 4) * PLANE + me)

    def in_plane(j):
        return (g, h * PLANE + (me + j) % PLANE)

    def block_of(beta):
        return beta + side * (3 - 2 * beta)

    def load(beta):
        return pltpu.make_async_copy(
            grads_ref.at[pl.ds(block_of(beta) * PER, PER)], gv[beta], g_sem.at[beta])

    for beta in (0, 1, 3, 2):
        load(beta).start()

    barrier = pltpu.get_barrier_semaphore()
    for hop in (dirn, -dirn, -2 * dirn):
        pl.semaphore_signal(barrier, inc=1, device_id=along_z(hop), device_id_type=MESH)

    @pl.when(inner)
    def _():
        pl.semaphore_signal(barrier, inc=1, device_id=along_z(4), device_id_type=MESH)

    def greet(j, carry):
        pl.semaphore_signal(barrier, inc=1, device_id=in_plane(j), device_id_type=MESH)
        return carry

    lax.fori_loop(1, PLANE, greet, 0)

    def remote(src, dst, send, recv, hop):
        return pltpu.make_async_remote_copy(
            src_ref=src, dst_ref=dst, send_sem=send, recv_sem=recv,
            device_id=along_z(hop), device_id_type=MESH)

    def part(ref, flow, n, k):
        return ref.at[n, k, pl.ds(0, size(flow))]

    def send_a(n, k):
        flow = ORIGIN[n]
        return remote(part(own, flow, n, k), part(a, flow, n, k), a_s.at[n, k], a_r.at[n, k], dirn)

    def send_b(n, k):
        flow = ORIGIN[n]
        return remote(part(a, flow, n, k), part(b, flow, n, k), b_s.at[n, k], b_r.at[n, k], dirn)

    def send_c(n, k):
        flow = BACK[n]
        return remote(part(b, flow, n, k), part(c, flow, n, k), c_s.at[n, k], c_r.at[n, k], -dirn)

    def send_x(n, k):
        count = pl.ds(0, size(BACK[n]))
        return remote(c.at[n, k, count], xf.at[k, count], x_s.at[n, k], x_r.at[k], -(n + 1) * dirn)

    def send_u(k):
        both = pl.ds(SURE, FULL - SURE)
        return remote(sf.at[k, both], xf.at[k, both], u_s.at[k], u_r.at[k], 4)

    def gather(n):
        kind, beta = LISTS[n]
        row = block_of(beta) * HALVES + h + kind * (1 - 2 * h)
        src = gv[beta]

        def body(i, carry):
            value = src[tab_ref[row, i]]
            for k in range(CHUNKS):
                r, q = k // 2, k % 2
                own[n, k, i] = value[r * TR:(r + 1) * TR, q * TC:(q + 1) * TC]
            return carry

        lax.fori_loop(0, size(LISTS[n]), body, 0, unroll=4)

    for n in range(len(LISTS)):
        if n in (0, 1, 2, 3):
            load(LISTS[n][1]).wait()
        gather(n)
        if n == 0:
            @pl.when(outer)
            def _():
                pl.semaphore_wait(barrier, 3 + PLANE - 1)

            @pl.when(inner)
            def _():
                pl.semaphore_wait(barrier, 4 + PLANE - 1)
        if n < len(ORIGIN):
            @pl.when(outer)
            def _():
                send_a(n, 0).start()

    def add(n, dst, srcs):
        count = size(LISTS[n])
        lanes = pl.ds(0, count)

        def total(k):
            value = own[n, k, lanes].astype(jnp.float32)
            for src, m in srcs:
                value += src[m, k, lanes].astype(jnp.float32)
            return value.astype(jnp.bfloat16)

        return total

    def spread(j, k):
        p = (me + j) % PLANE
        return pltpu.make_async_remote_copy(
            src_ref=dsp.at[k, p], dst_ref=out_ref.at[:, k // 2, k % 2, me],
            send_sem=p_s.at[j], recv_sem=p_r.at[me], device_id=in_plane(j), device_id_type=MESH)

    def step(k, carry):
        @pl.when(outer)
        def _():
            @pl.when(k + 1 < CHUNKS)
            def _():
                for n in range(len(ORIGIN)):
                    send_a(n, k + 1).start()

            for n, flow in enumerate(BACK):
                send_c(n, k).wait_recv()
                total = add(5 + n, None, [(c, n)])(k)
                if n < 2:
                    c[n, k, pl.ds(0, size(flow))] = total
                    send_x(n, k).start()
                else:
                    sf[k] = total
            send_x(0, k).wait_recv()

        @pl.when(inner)
        def _():
            def forward(n):
                send_a(n, k).wait_recv()
                a[n, k, pl.ds(0, size(ORIGIN[n]))] = add(n, None, [(a, n)])(k)
                send_b(n, k).start()

            def back(n):
                send_b(n, k).wait_recv()
                b[n, k, pl.ds(0, size(BACK[n]))] = add(5 + n, None, [(b, n)])(k)
                send_c(n, k).start()

            forward(0)
            forward(1)
            back(0)
            forward(2)
            back(1)
            forward(3)
            back(2)
            send_a(4, k).wait_recv()
            send_b(3, k).wait_recv()
            sf[k] = add(4, None, [(a, 4), (b, 3)])(k)
            send_u(k).start()
            send_x(1, k).wait_recv()
            send_u(k).wait_recv()

        xs[...] = xf[k]

        def fill(j, carry):
            p = (me + j) % PLANE
            for s in range(CAP):
                i = tab_ref[8 + s, h * PLANE + p]
                dsp[k, p, s, h] = sf[k, i]
                dsp[k, p, s, 1 - h] = xs[i]
            spread(j, k).start()
            return carry

        lax.fori_loop(1, PLANE, fill, 0)
        for s in range(CAP):
            i = tab_ref[8 + s, h * PLANE + me]
            dsp[k, me, s, h] = sf[k, i]
            dsp[k, me, s, 1 - h] = xs[i]
        pltpu.make_async_copy(
            dsp.at[k, me], out_ref.at[:, k // 2, k % 2, me], p_r.at[me]).start()
        return carry

    lax.fori_loop(0, CHUNKS, step, 0)

    def finish(k, carry):
        @pl.when(outer)
        def _():
            for n in range(5):
                send_a(n, k).wait_send()
            for n in range(2):
                send_x(n, k).wait_send()

        @pl.when(inner)
        def _():
            for n in range(4):
                send_b(n, k).wait_send()
            for n in range(3):
                send_c(n, k).wait_send()
            send_u(k).wait_send()

        return carry

    lax.fori_loop(0, CHUNKS, finish, 0)

    def sent(j, carry):
        whole = dsp.at[:, (me + j) % PLANE]
        pltpu.make_async_copy(whole, whole, p_s.at[j]).wait()
        return carry

    lax.fori_loop(1, PLANE, sent, 0)

    def landed(src, carry):
        whole = out_ref.at[:, :, :, src]
        pltpu.make_async_copy(whole, whole, p_r.at[src]).wait()
        return carry

    lax.fori_loop(0, PLANE, landed, 0)


def run_exchange(tab, owner, grads):
    rows, cols = grads.shape[1:]
    dma = pltpu.SemaphoreType.DMA
    vmem = lambda *shape: pltpu.VMEM(shape, jnp.bfloat16)
    return pl.pallas_call(
        exchange,
        out_shape=jax.ShapeDtypeStruct((CAP, 2, 2, PLANE, HALVES, TR, TC), jnp.bfloat16),
        in_specs=[
            pl.BlockSpec(memory_space=pltpu.SMEM),
            pl.BlockSpec(memory_space=pl.ANY),
        ],
        out_specs=pl.BlockSpec(memory_space=pl.ANY),
        scratch_shapes=[
            *[vmem(PER, rows, cols) for _ in range(4)],
            vmem(8, CHUNKS, FULL, TR, TC),
            vmem(5, CHUNKS, FULL, TR, TC),
            vmem(4, CHUNKS, FULL, TR, TC),
            vmem(3, CHUNKS, FULL, TR, TC),
            vmem(CHUNKS, FULL, TR, TC),
            vmem(FULL, TR, TC),
            vmem(CHUNKS, FULL, TR, TC),
            vmem(CHUNKS, PLANE, CAP, HALVES, TR, TC),
            dma((4,)),
            dma((5, CHUNKS)), dma((5, CHUNKS)),
            dma((4, CHUNKS)), dma((4, CHUNKS)),
            dma((3, CHUNKS)), dma((3, CHUNKS)),
            dma((2, CHUNKS)), dma((CHUNKS,)),
            dma((CHUNKS,)), dma((CHUNKS,)),
            dma((PLANE,)), dma((PLANE,)),
        ],
        compiler_params=pltpu.CompilerParams(
            collective_id=1, has_side_effects=True, vmem_limit_bytes=48 * 2**20),
        name="exchange",
    )(tab, grads)


def run_any(tab, owner, grads):
    rows, cols = grads.shape[1:]
    parts = lax.all_to_all(grads, "dp", split_axis=0, concat_axis=0, tiled=True)
    parts = parts.reshape(-1, PER, rows, cols).astype(jnp.float32)
    summed = jnp.sum(parts, axis=0).astype(jnp.bfloat16)
    own = lax.dynamic_slice_in_dim(owner, lax.axis_index("dp") * PER, PER)
    index = jnp.arange(PER, dtype=jnp.int32)
    same = own[None, :] == own[:, None]
    slot = jnp.sum((same & (index[None, :] < index[:, None])).astype(jnp.int32), axis=1)
    hit = (slot[None, None, :] == jnp.arange(CAP)[:, None, None]) & (
        own[None, None, :] == jnp.arange(HALVES * PLANE)[None, :, None])
    sends = jnp.einsum(
        "sdj,jrc->sdrc", hit.astype(jnp.bfloat16), summed, preferred_element_type=jnp.float32
    ).astype(jnp.bfloat16)
    got = lax.all_to_all(sends, "fsdp", split_axis=1, concat_axis=1, tiled=True)
    got = got.reshape(CAP, HALVES, PLANE, 2, TR, 2, TC)
    return got.transpose(0, 3, 5, 2, 1, 4, 6)


def newton(scale_out, tab_ref, x_ref, out_ref):
    cols = 2 * TC
    half_rows = PLANE * HALVES * TR
    f32 = jnp.float32
    row = lax.broadcasted_iota(jnp.int32, (cols, cols), 0)
    col = lax.broadcasted_iota(jnp.int32, (cols, cols), 1)
    eye = (row == col).astype(f32)
    live = tab_ref[10, lax.axis_index("fsdp")]

    def dot(p, q):
        return jnp.dot(p.astype(jnp.bfloat16), q.astype(jnp.bfloat16), preferred_element_type=f32)

    def half(s, r):
        return jnp.concatenate(
            [x_ref[s, r, c].reshape(half_rows, TC) for c in range(2)], axis=1)

    grams, maps, scales = [], [], []
    for s in range(CAP):
        gram = jnp.zeros((cols, cols), f32)
        for r in range(2):
            part = half(s, r)
            gram += lax.dot_general(part, part, (((0,), (0,)), ((), ())), preferred_element_type=f32)
        norm = jnp.sqrt(jnp.sum(gram * eye, keepdims=True))
        inv = 1.0 / (norm + 1e-07)
        grams.append(gram * inv * inv)
        scales.append(inv * scale_out)
        maps.append(None)
    for it in range(3):
        for s in range(CAP):
            gram = grams[s]
            poly = 3.4445 * eye - 4.775 * gram + 2.0315 * dot(gram, gram)
            maps[s] = poly if maps[s] is None else dot(maps[s], poly)
            if it < 2:
                grams[s] = dot(poly, dot(gram, poly))
    for s in range(CAP):
        last = (maps[s] * scales[s]).astype(jnp.bfloat16)
        for r in range(2):
            y = jnp.dot(half(s, r), last, preferred_element_type=f32)
            y = jnp.where(s < live, y, 0.0).astype(jnp.bfloat16)
            y = y.reshape(PLANE, HALVES, TR, cols)
            for hh in range(HALVES):
                out_ref[s, hh, :, r] = y[:, hh]


def tables(owner_ref, tab_ref):
    f32 = jnp.float32
    g = lax.axis_index("dp")
    h = lax.axis_index("fsdp") // PLANE
    groups = owner_ref.shape[1] // PER
    owner = jnp.concatenate([owner_ref[:, b * PER:(b + 1) * PER] for b in range(groups)], axis=0)
    sub = lax.broadcasted_iota(jnp.int32, (PER, PER), 0)
    lane = lax.broadcasted_iota(jnp.int32, (PER, PER), 1)
    before = (sub < lane).astype(f32)
    index = lax.broadcasted_iota(jnp.int32, (groups, PER), 1).astype(f32)
    far = (owner >= PLANE).astype(f32)
    ones_before = jnp.dot(far, before, preferred_element_type=f32)
    near_count = PER - jnp.sum(far, axis=1, keepdims=True)
    order = jnp.where(far > 0, near_count + ones_before, index - ones_before)
    key = jnp.where(order >= FULL, order - FULL, jnp.where(order >= SURE, order, -1.0))
    subf = sub.astype(f32)
    weight = lax.broadcasted_iota(jnp.int32, (8, PER), 1).astype(f32)

    def rowdot(left, hot):
        out = lax.dot_general(left, hot, (((1,), (1,)), ((), ())), preferred_element_type=f32)
        return out[0:1].astype(jnp.int32)

    tab_ref[...] = jnp.zeros_like(tab_ref)
    for blk in range(groups):
        for half, keys in enumerate((order, key)):
            hot = (keys[blk:blk + 1] == subf).astype(f32)
            tab_ref[2 * blk + half:2 * blk + half + 1, 0:PER] = rowdot(weight, hot)
    mine = lax.broadcasted_iota(jnp.int32, (groups, PER), 0) == g
    own = jnp.sum(jnp.where(mine, owner, 0), axis=0, keepdims=True)
    place = jnp.sum(jnp.where(mine, jnp.where(h == 0, order, key), 0.0), axis=0, keepdims=True)
    has = (own == sub).astype(f32)
    slot = jnp.sum(has * jnp.dot(has, before, preferred_element_type=f32), axis=0, keepdims=True)
    place = jnp.broadcast_to(place, (8, PER))
    for s in range(CAP):
        tab_ref[8 + s:9 + s, 0:PER] = rowdot(place, has * (slot == s).astype(f32))
    tab_ref[10:11, 0:PER] = rowdot(jnp.ones((8, PER), f32), has)
    good = (near_count >= SURE) & (near_count <= FULL)
    good = jnp.min(good.astype(f32), axis=0, keepdims=True).astype(jnp.int32)
    tab_ref[11:12, 0:PER] = jnp.broadcast_to(good, (1, PER))


def per_device(grads, owner):
    local = grads[0]
    mats, rows, cols = local.shape
    scale_out = 0.2 * math.sqrt(max(rows * PLANE * HALVES, cols))
    tab = pl.pallas_call(
        tables,
        out_shape=jax.ShapeDtypeStruct((16, 128), jnp.int32),
        in_specs=[pl.BlockSpec(memory_space=pltpu.VMEM)],
        out_specs=pl.BlockSpec(memory_space=pltpu.VMEM),
        name="tables",
    )(owner.reshape(1, mats))
    gathered = lax.cond(tab[11, 0] == 1, run_exchange, run_any, tab, owner, local)
    owned = pl.pallas_call(
        functools.partial(newton, scale_out),
        out_shape=jax.ShapeDtypeStruct((CAP, HALVES, PLANE, 2, TR, cols), jnp.bfloat16),
        in_specs=[pl.BlockSpec(memory_space=pltpu.SMEM), pl.BlockSpec(memory_space=pltpu.VMEM)],
        out_specs=pl.BlockSpec(memory_space=pltpu.VMEM),
        compiler_params=pltpu.CompilerParams(vmem_limit_bytes=48 * 2**20),
        name="newton",
    )(tab, gathered)
    return owned.reshape(1, 1, CAP, HALVES * PLANE * rows, cols)


def solution(mesh):
    placed = (P("dp", None, "fsdp", None), P())
    return jax.shard_map(
        per_device,
        mesh=mesh,
        in_specs=placed,
        out_specs=P("dp", "fsdp", None, None, None),
        check_vma=False,
    )
```

```python
import functools
import math

import jax
import jax.numpy as jnp
from jax import lax
from jax.experimental import pallas as pl
from jax.experimental.pallas import tpu as pltpu
from jax.sharding import PartitionSpec as P

MESH = pl.DeviceIdType.MESH
CAP = 2
HALVES = 2
PLANE = 32
CHUNKS = 4
TR, TC = 16, 128
PER = 64
SURES = (28, 25, 20)
ORIGIN = ((1, 0), (1, 1), (0, 3), (0, 2), (0, 1))
LISTS = ORIGIN + ((1, 3), (1, 2), (0, 0))
GATHER = ((1, (0,)), (0, (1, 2)), (3, ()), (4, (3, 4)), (2, (5, 6, 7)), (5, ()), (6, ()), (7, ()))
ONWARD = (0, 1, 2, 3, 5, 6, 7)
HOME = (0, 1, 2, 5, 6)
FAR = (0, 1, 2)


def layout(sure):
    full = PER - sure
    half = full // 2
    return ((1, 0, sure), (0, 0, half), (0, half, full), (3, sure, full), (4, sure, full),
            (2, 0, half), (2, half, full), (3, 0, sure), (4, 0, sure))


def exchange(sure, tab_ref, grads_ref, out_ref, g0, g1, g2, g3, own, a, b, c, xf, xs, sf, dsp,
             g_sem, a_s, a_r, b_s, b_r, c_s, c_r, x_s, x_r, u_s, u_r, p_s, p_r):
    pieces_of = layout(sure)
    full = PER - sure
    gv = (g0, g1, g2, g3)
    g = lax.axis_index("dp")
    f = lax.axis_index("fsdp")
    h, me = f // PLANE, f % PLANE
    z = h * 4 + g
    side = g // 2
    dirn = 1 - 2 * side
    outer = (g == 0) | (g == 3)
    inner = jnp.logical_not(outer)

    def along_z(step):
        zz = (z + step + 16) % 8
        return (zz % 4, (zz // 4) * PLANE + me)

    def in_plane(j):
        return (g, h * PLANE + (me + j) % PLANE)

    def block_of(beta):
        return beta + side * (3 - 2 * beta)

    def load(beta):
        return pltpu.make_async_copy(
            grads_ref.at[pl.ds(block_of(beta) * PER, PER)], gv[beta], g_sem.at[beta])

    for beta in (1, 0, 2, 3):
        load(beta).start()

    barrier = pltpu.get_barrier_semaphore()
    for hop in (dirn, -dirn, -2 * dirn):
        pl.semaphore_signal(barrier, inc=1, device_id=along_z(hop), device_id_type=MESH)

    @pl.when(inner)
    def _():
        pl.semaphore_signal(barrier, inc=1, device_id=along_z(4), device_id_type=MESH)

    def greet(j, carry):
        pl.semaphore_signal(barrier, inc=1, device_id=in_plane(j), device_id_type=MESH)
        return carry

    lax.fori_loop(1, PLANE, greet, 0)

    def remote(src, dst, send, recv, hop):
        return pltpu.make_async_remote_copy(
            src_ref=src, dst_ref=dst, send_sem=send, recv_sem=recv,
            device_id=along_z(hop), device_id_type=MESH)

    def part(ref, m, k):
        n, low, high = pieces_of[m]
        return ref.at[n, k, pl.ds(low, high - low)]

    def send_a(m, k):
        return remote(part(own, m, k), part(a, m, k), a_s.at[m, k], a_r.at[m, k], dirn)

    def send_b(m, k):
        return remote(part(a, m, k), part(b, m, k), b_s.at[m, k], b_r.at[m, k], dirn)

    def send_c(m, k):
        return remote(part(b, m, k), part(c, m, k), c_s.at[m, k], c_r.at[m, k], -dirn)

    def send_x(m, k):
        n, low, high = pieces_of[m]
        lanes = pl.ds(low, high - low)
        return remote(c.at[n, k, lanes], xf.at[k, lanes], x_s.at[m, k], x_r.at[m, k], (-1 - n) * dirn)

    def send_u(k):
        both = pl.ds(sure, full - sure)
        return remote(sf.at[k, both], xf.at[k, both], u_s.at[k], u_r.at[k], 4)

    def gather(n):
        kind, beta = LISTS[n]
        row = block_of(beta) * HALVES + h + kind * (1 - 2 * h)
        src = gv[beta]

        def body(i, carry):
            value = src[tab_ref[row, i]]
            for k in range(CHUNKS):
                r, q = k // 2, k % 2
                own[n, k, i] = value[r * TR:(r + 1) * TR, q * TC:(q + 1) * TC]
            return carry

        count = sure if LISTS[n] in ((1, 1), (1, 2)) else full
        lax.fori_loop(0, count, body, 0, unroll=4)

    def start_a(n, k):
        @pl.when(outer)
        def _():
            send_a(n, k).start()

    loaded = []
    for turn, (n, pieces) in enumerate(GATHER):
        if LISTS[n][1] not in loaded:
            load(LISTS[n][1]).wait()
            loaded.append(LISTS[n][1])
        gather(n)
        if turn == 0:
            @pl.when(outer)
            def _():
                pl.semaphore_wait(barrier, 3 + PLANE - 1)

            @pl.when(inner)
            def _():
                pl.semaphore_wait(barrier, 4 + PLANE - 1)
        for m in pieces:
            start_a(m, 0)

    def total(mine, m, k, *srcs):
        _, low, high = pieces_of[m]
        lanes = pl.ds(low, high - low)
        value = own[mine, k, lanes].astype(jnp.float32)
        for src, n in srcs:
            value += src[n, k, lanes].astype(jnp.float32)
        return value.astype(jnp.bfloat16)

    def spread(j, k, kind):
        p = (me + j) % PLANE
        return pltpu.make_async_remote_copy(
            src_ref=dsp.at[k, kind, p],
            dst_ref=out_ref.at[:, k // 2, k % 2, me, h + kind * (1 - 2 * h)],
            send_sem=p_s.at[j], recv_sem=p_r.at[me], device_id=in_plane(j), device_id_type=MESH)

    def dispatch(k, kind):
        def fill(p):
            for s in range(CAP):
                i = tab_ref[8 + s, h * PLANE + p]
                dsp[k, kind, p, s] = xs[i] if kind else sf[k, i]

        def body(j, carry):
            fill((me + j) % PLANE)
            spread(j, k, kind).start()
            return carry

        lax.fori_loop(1, PLANE, body, 0)
        fill(me)
        pltpu.make_async_copy(
            dsp.at[k, kind, me], out_ref.at[:, k // 2, k % 2, me, h + kind * (1 - 2 * h)],
            p_r.at[me]).start()

    def step(t, carry):
        k = t - 1

        def ahead(*runs):
            @pl.when(t < CHUNKS)
            def _():
                for run, *args in runs:
                    run(*args)

        def behind(*runs):
            @pl.when(t >= 1)
            def _():
                for run, *args in runs:
                    run(*args)

        def from_far(*pieces):
            for m in pieces:
                send_x(m, k).wait_recv()
            xs[...] = xf[k]
            dispatch(k, 1)

        @pl.when(outer)
        def _():
            @pl.when(t + 1 < CHUNKS)
            def _():
                for m in range(8):
                    send_a(m, t + 1).start()

            @pl.when(t < CHUNKS)
            def _():
                send_a(8, t).start()

            def back(m):
                send_c(m, t).wait_recv()
                n, low, high = pieces_of[m]
                c[n, t, pl.ds(low, high - low)] = total(5 + n, m, t, (c, n))
                send_x(m, t).start()

            def last(m):
                send_c(m, k).wait_recv()
                _, low, high = pieces_of[m]
                sf[k, pl.ds(low, high - low)] = total(7, m, k, (c, 2))

            behind((from_far, 1, 2), (last, 5), (last, 6), (dispatch, k, 0))
            ahead((back, 0), (back, 1), (back, 2))

        @pl.when(inner)
        def _():
            def forward(m):
                send_a(m, t).wait_recv()
                n, low, high = pieces_of[m]
                a[n, t, pl.ds(low, high - low)] = total(n, m, t, (a, n))
                send_b(m, t).start()

            def back(m):
                send_b(m, t).wait_recv()
                n, low, high = pieces_of[m]
                b[n, t, pl.ds(low, high - low)] = total(5 + n, m, t, (b, n))
                send_c(m, t).start()

            def last(m, across, q):
                send_a(m, q).wait_recv()
                send_b(across, q).wait_recv()
                _, low, high = pieces_of[m]
                sf[q, pl.ds(low, high - low)] = total(4, m, q, (a, 4), (b, 3))

            def both():
                last(4, 3, t)
                send_u(t).start()

            def arrive():
                send_u(k).wait_recv()
                from_far(0)

            behind((arrive,))
            ahead((forward, 0), (forward, 1), (forward, 2), (back, 0), (forward, 3), (back, 1),
                  (back, 2), (forward, 5), (both,), (forward, 6), (forward, 7), (back, 5))
            behind((last, 8, 7, k))
            ahead((back, 6))
            behind((dispatch, k, 0))

        return carry

    lax.fori_loop(0, CHUNKS + 1, step, 0)

    def finish(k, carry):
        @pl.when(outer)
        def _():
            for m in range(9):
                send_a(m, k).wait_send()
            for m in FAR:
                send_x(m, k).wait_send()

        @pl.when(inner)
        def _():
            for m in ONWARD:
                send_b(m, k).wait_send()
            for m in HOME:
                send_c(m, k).wait_send()
            send_u(k).wait_send()

        return carry

    lax.fori_loop(0, CHUNKS, finish, 0)

    def sent(j, carry):
        whole = dsp.at[:, :, (me + j) % PLANE]
        pltpu.make_async_copy(whole, whole, p_s.at[j]).wait()
        return carry

    lax.fori_loop(1, PLANE, sent, 0)

    def landed(src, carry):
        whole = out_ref.at[:, :, :, src]
        pltpu.make_async_copy(whole, whole, p_r.at[src]).wait()
        return carry

    lax.fori_loop(0, PLANE, landed, 0)


def run_exchange(ident, sure, tab, owner, grads):
    full = PER - sure
    rows, cols = grads.shape[1:]
    dma = pltpu.SemaphoreType.DMA
    vmem = lambda *shape: pltpu.VMEM(shape, jnp.bfloat16)
    return pl.pallas_call(
        functools.partial(exchange, sure),
        out_shape=jax.ShapeDtypeStruct((CAP, 2, 2, PLANE, HALVES, TR, TC), jnp.bfloat16),
        in_specs=[
            pl.BlockSpec(memory_space=pltpu.SMEM),
            pl.BlockSpec(memory_space=pl.ANY),
        ],
        out_specs=pl.BlockSpec(memory_space=pl.ANY),
        scratch_shapes=[
            *[vmem(PER, rows, cols) for _ in range(4)],
            vmem(8, CHUNKS, full, TR, TC),
            vmem(5, CHUNKS, full, TR, TC),
            vmem(4, CHUNKS, full, TR, TC),
            vmem(3, CHUNKS, full, TR, TC),
            vmem(CHUNKS, full, TR, TC),
            vmem(full, TR, TC),
            vmem(CHUNKS, full, TR, TC),
            vmem(CHUNKS, HALVES, PLANE, CAP, TR, TC),
            dma((4,)),
            dma((9, CHUNKS)), dma((9, CHUNKS)),
            dma((9, CHUNKS)), dma((9, CHUNKS)),
            dma((9, CHUNKS)), dma((9, CHUNKS)),
            dma((3, CHUNKS)), dma((3, CHUNKS)),
            dma((CHUNKS,)), dma((CHUNKS,)),
            dma((PLANE,)), dma((PLANE,)),
        ],
        compiler_params=pltpu.CompilerParams(
            collective_id=ident, has_side_effects=True, vmem_limit_bytes=48 * 2**20),
        name=f"exchange{sure}",
    )(tab, grads)


def run_any(tab, owner, grads):
    rows, cols = grads.shape[1:]
    parts = lax.all_to_all(grads, "dp", split_axis=0, concat_axis=0, tiled=True)
    parts = parts.reshape(-1, PER, rows, cols).astype(jnp.float32)
    summed = jnp.sum(parts, axis=0).astype(jnp.bfloat16)
    own = lax.dynamic_slice_in_dim(owner, lax.axis_index("dp") * PER, PER)
    index = jnp.arange(PER, dtype=jnp.int32)
    same = own[None, :] == own[:, None]
    slot = jnp.sum((same & (index[None, :] < index[:, None])).astype(jnp.int32), axis=1)
    hit = (slot[None, None, :] == jnp.arange(CAP)[:, None, None]) & (
        own[None, None, :] == jnp.arange(HALVES * PLANE)[None, :, None])
    sends = jnp.einsum(
        "sdj,jrc->sdrc", hit.astype(jnp.bfloat16), summed, preferred_element_type=jnp.float32
    ).astype(jnp.bfloat16)
    got = lax.all_to_all(sends, "fsdp", split_axis=1, concat_axis=1, tiled=True)
    got = got.reshape(CAP, HALVES, PLANE, 2, TR, 2, TC)
    return got.transpose(0, 3, 5, 2, 1, 4, 6)


def newton(scale_out, tab_ref, x_ref, out_ref, y_ref, sems):
    cols = 2 * TC
    half_rows = PLANE * HALVES * TR
    f32 = jnp.float32
    row = lax.broadcasted_iota(jnp.int32, (cols, cols), 0)
    col = lax.broadcasted_iota(jnp.int32, (cols, cols), 1)
    eye = (row == col).astype(f32)
    live = tab_ref[10, lax.axis_index("fsdp")]

    def dot(p, q):
        return jnp.dot(p.astype(jnp.bfloat16), q.astype(jnp.bfloat16), preferred_element_type=f32)

    def half(s, r):
        return jnp.concatenate(
            [x_ref[s, r, c].reshape(half_rows, TC) for c in range(2)], axis=1)

    grams, maps, scales = [], [], []
    for s in range(CAP):
        gram = jnp.zeros((cols, cols), f32)
        for r in range(2):
            part = half(s, r)
            gram += lax.dot_general(part, part, (((0,), (0,)), ((), ())), preferred_element_type=f32)
        norm = jnp.sqrt(jnp.sum(gram * eye, keepdims=True))
        inv = 1.0 / (norm + 1e-07)
        grams.append(gram * inv * inv)
        scales.append(inv * scale_out)
        maps.append(None)
    for it in range(3):
        for s in range(CAP):
            gram = grams[s]
            poly = 3.4445 * eye - 4.775 * gram + 2.0315 * dot(gram, gram)
            maps[s] = poly if maps[s] is None else dot(maps[s], poly)
            if it < 2:
                grams[s] = dot(poly, dot(gram, poly))
    for s in range(CAP):
        last = (maps[s] * scales[s]).astype(jnp.bfloat16)
        for r in range(2):
            y = jnp.dot(half(s, r), last, preferred_element_type=f32)
            y = jnp.where(s < live, y, 0.0).astype(jnp.bfloat16)
            y = y.reshape(PLANE, HALVES, TR, cols)
            for hh in range(HALVES):
                y_ref[s, r, hh] = y[:, hh]
            pltpu.make_async_copy(y_ref.at[s, r], out_ref.at[s, :, :, r], sems.at[s, r]).start()
    for s in range(CAP):
        for r in range(2):
            pltpu.make_async_copy(y_ref.at[s, r], out_ref.at[s, :, :, r], sems.at[s, r]).wait()


def tables(owner_ref, tab_ref):
    f32 = jnp.float32
    g = lax.axis_index("dp")
    h = lax.axis_index("fsdp") // PLANE
    groups = owner_ref.shape[1] // PER
    owner = jnp.concatenate([owner_ref[:, b * PER:(b + 1) * PER] for b in range(groups)], axis=0)
    sub = lax.broadcasted_iota(jnp.int32, (PER, PER), 0)
    lane = lax.broadcasted_iota(jnp.int32, (PER, PER), 1)
    before = (sub < lane).astype(f32)
    index = lax.broadcasted_iota(jnp.int32, (groups, PER), 1).astype(f32)
    far = (owner >= PLANE).astype(f32)
    ones_before = jnp.dot(far, before, preferred_element_type=f32)
    near_count = PER - jnp.sum(far, axis=1, keepdims=True)
    order = jnp.where(far > 0, near_count + ones_before, index - ones_before)
    fewest = jnp.min(jnp.minimum(near_count, PER - near_count), axis=0, keepdims=True)
    sure, tier = jnp.full((1, 1), float(SURES[-1]), f32), jnp.full((1, 1), float(len(SURES)), f32)
    for number, count in reversed(tuple(enumerate(SURES))):
        sure = jnp.where(fewest >= count, float(count), sure)
        tier = jnp.where(fewest >= count, float(number), tier)
    key = jnp.where(order >= PER - sure, order - (PER - sure), jnp.where(order >= sure, order, -1.0))
    subf = sub.astype(f32)
    weight = lax.broadcasted_iota(jnp.int32, (8, PER), 1).astype(f32)

    def rowdot(left, hot):
        out = lax.dot_general(left, hot, (((1,), (1,)), ((), ())), preferred_element_type=f32)
        return out[0:1].astype(jnp.int32)

    tab_ref[...] = jnp.zeros_like(tab_ref)
    for blk in range(groups):
        for half, keys in enumerate((order, key)):
            hot = (keys[blk:blk + 1] == subf).astype(f32)
            tab_ref[2 * blk + half:2 * blk + half + 1, 0:PER] = rowdot(weight, hot)
    mine = lax.broadcasted_iota(jnp.int32, (groups, PER), 0) == g
    own = jnp.sum(jnp.where(mine, owner, 0), axis=0, keepdims=True)
    place = jnp.sum(jnp.where(mine, jnp.where(h == 0, order, key), 0.0), axis=0, keepdims=True)
    has = (own == sub).astype(f32)
    slot = jnp.sum(has * jnp.dot(has, before, preferred_element_type=f32), axis=0, keepdims=True)
    place = jnp.broadcast_to(place, (8, PER))
    for s in range(CAP):
        tab_ref[8 + s:9 + s, 0:PER] = rowdot(place, has * (slot == s).astype(f32))
    tab_ref[10:11, 0:PER] = rowdot(jnp.ones((8, PER), f32), has)
    tab_ref[11:12, 0:PER] = jnp.broadcast_to(tier.astype(jnp.int32), (1, PER))


def per_device(grads, owner):
    local = grads[0]
    mats, rows, cols = local.shape
    scale_out = 0.2 * math.sqrt(max(rows * PLANE * HALVES, cols))
    tab = pl.pallas_call(
        tables,
        out_shape=jax.ShapeDtypeStruct((16, 128), jnp.int32),
        in_specs=[pl.BlockSpec(memory_space=pltpu.VMEM)],
        out_specs=pl.BlockSpec(memory_space=pltpu.VMEM),
        name="tables",
    )(owner.reshape(1, mats))
    ways = [functools.partial(run_exchange, 1 + n, sure) for n, sure in enumerate(SURES)]
    gathered = lax.switch(tab[11, 0], ways + [run_any], tab, owner, local)
    owned = pl.pallas_call(
        functools.partial(newton, scale_out),
        out_shape=jax.ShapeDtypeStruct((CAP, HALVES, PLANE, 2, TR, cols), jnp.bfloat16),
        in_specs=[pl.BlockSpec(memory_space=pltpu.SMEM), pl.BlockSpec(memory_space=pltpu.VMEM)],
        out_specs=pl.BlockSpec(memory_space=pl.ANY),
        scratch_shapes=[
            pltpu.VMEM((CAP, 2, HALVES, PLANE, TR, cols), jnp.bfloat16),
            pltpu.SemaphoreType.DMA((CAP, 2)),
        ],
        compiler_params=pltpu.CompilerParams(vmem_limit_bytes=48 * 2**20),
        name="newton",
    )(tab, gathered)
    return owned.reshape(1, 1, CAP, HALVES * PLANE * rows, cols)


def solution(mesh):
    placed = (P("dp", None, "fsdp", None), P())
    return jax.shard_map(
        per_device,
        mesh=mesh,
        in_specs=placed,
        out_specs=P("dp", "fsdp", None, None, None),
        check_vma=False,
    )
```

```python
import functools
import math

import jax
import jax.numpy as jnp
from jax import lax
from jax.experimental import pallas as pl
from jax.experimental.pallas import tpu as pltpu
from jax.sharding import PartitionSpec as P

MESH = pl.DeviceIdType.MESH
CAP = 2
HALVES = 2
PLANE = 32
CHUNKS = 4
TR, TC = 16, 128
PER = 64
SURES = (29, 27, 25, 20, 0)
ORIGIN = ((1, 0), (1, 1), (0, 3), (0, 2), (0, 1))
LISTS = ORIGIN + ((1, 3), (1, 2), (0, 0))
GATHER = ((1, (0,)), (0, (1, 2)), (3, ()), (4, (3, 4)), (2, (5, 6, 7)), (5, ()), (6, ()), (7, ()))
ONWARD = (0, 1, 2, 3, 5, 6, 7)
HOME = (0, 1, 2, 5, 6)
FAR = (0, 1, 2)


def layout(sure):
    full = PER - sure
    half = full // 2
    return ((1, 0, sure), (0, 0, half), (0, half, full), (3, sure, full), (4, sure, full),
            (2, 0, half), (2, half, full), (3, 0, sure), (4, 0, sure))


def exchange(sure, tab_ref, grads_ref, out_ref, g0, g1, g2, g3, own, a, b, c, xf, xs, sf, dsp,
             g_sem, a_s, a_r, b_s, b_r, c_s, c_r, x_s, x_r, u_s, u_r, p_s, p_r):
    pieces_of = layout(sure)
    full = PER - sure
    some = [high > low for _, low, high in pieces_of]
    gv = (g0, g1, g2, g3)
    g = lax.axis_index("dp")
    f = lax.axis_index("fsdp")
    h, me = f // PLANE, f % PLANE
    z = h * 4 + g
    side = g // 2
    dirn = 1 - 2 * side
    outer = (g == 0) | (g == 3)
    inner = jnp.logical_not(outer)

    def along_z(step):
        zz = (z + step + 16) % 8
        return (zz % 4, (zz // 4) * PLANE + me)

    def in_plane(j):
        return (g, h * PLANE + (me + j) % PLANE)

    def block_of(beta):
        return beta + side * (3 - 2 * beta)

    def load(beta):
        return pltpu.make_async_copy(
            grads_ref.at[pl.ds(block_of(beta) * PER, PER)], gv[beta], g_sem.at[beta])

    for beta in (1, 0, 2, 3):
        load(beta).start()

    barrier = pltpu.get_barrier_semaphore()
    for hop in (dirn, -dirn, -2 * dirn):
        pl.semaphore_signal(barrier, inc=1, device_id=along_z(hop), device_id_type=MESH)

    @pl.when(inner)
    def _():
        pl.semaphore_signal(barrier, inc=1, device_id=along_z(4), device_id_type=MESH)

    def greet(j, carry):
        pl.semaphore_signal(barrier, inc=1, device_id=in_plane(j), device_id_type=MESH)
        return carry

    lax.fori_loop(1, PLANE, greet, 0)

    def remote(src, dst, send, recv, hop):
        return pltpu.make_async_remote_copy(
            src_ref=src, dst_ref=dst, send_sem=send, recv_sem=recv,
            device_id=along_z(hop), device_id_type=MESH)

    def part(ref, m, k):
        n, low, high = pieces_of[m]
        return ref.at[n, k, pl.ds(low, high - low)]

    def send_a(m, k):
        return remote(part(own, m, k), part(a, m, k), a_s.at[m, k], a_r.at[m, k], dirn)

    def send_b(m, k):
        return remote(part(a, m, k), part(b, m, k), b_s.at[m, k], b_r.at[m, k], dirn)

    def send_c(m, k):
        return remote(part(b, m, k), part(c, m, k), c_s.at[m, k], c_r.at[m, k], -dirn)

    def send_x(m, k):
        n, low, high = pieces_of[m]
        lanes = pl.ds(low, high - low)
        return remote(c.at[n, k, lanes], xf.at[k, lanes], x_s.at[m, k], x_r.at[m, k], (-1 - n) * dirn)

    def send_u(k):
        both = pl.ds(sure, full - sure)
        return remote(sf.at[k, both], xf.at[k, both], u_s.at[k], u_r.at[k], 4)

    def gather(n):
        kind, beta = LISTS[n]
        row = block_of(beta) * HALVES + h + kind * (1 - 2 * h)
        src = gv[beta]

        def body(i, carry):
            value = src[tab_ref[row, i]]
            for k in range(CHUNKS):
                r, q = k // 2, k % 2
                own[n, k, i] = value[r * TR:(r + 1) * TR, q * TC:(q + 1) * TC]
            return carry

        count = sure if LISTS[n] in ((1, 1), (1, 2)) else full
        if count:
            lax.fori_loop(0, count, body, 0, unroll=4)

    def start_a(n, k):
        @pl.when(outer)
        def _():
            send_a(n, k).start()

    loaded = []
    for turn, (n, pieces) in enumerate(GATHER):
        if LISTS[n][1] not in loaded:
            load(LISTS[n][1]).wait()
            loaded.append(LISTS[n][1])
        gather(n)
        if turn == 0:
            @pl.when(outer)
            def _():
                pl.semaphore_wait(barrier, 3 + PLANE - 1)

            @pl.when(inner)
            def _():
                pl.semaphore_wait(barrier, 4 + PLANE - 1)
        for m in pieces:
            if some[m]:
                start_a(m, 0)

    def total(mine, m, k, *srcs):
        _, low, high = pieces_of[m]
        lanes = pl.ds(low, high - low)
        value = own[mine, k, lanes].astype(jnp.float32)
        for src, n in srcs:
            value += src[n, k, lanes].astype(jnp.float32)
        return value.astype(jnp.bfloat16)

    def spread(j, k, kind):
        p = (me + j) % PLANE
        return pltpu.make_async_remote_copy(
            src_ref=dsp.at[k, kind, p],
            dst_ref=out_ref.at[:, k // 2, k % 2, me, h + kind * (1 - 2 * h)],
            send_sem=p_s, recv_sem=p_r, device_id=in_plane(j), device_id_type=MESH)

    def dispatch(k, kind):
        def fill(p):
            for s in range(CAP):
                i = tab_ref[8 + s, h * PLANE + p]
                dsp[k, kind, p, s] = xs[i] if kind else sf[k, i]

        def body(j, carry):
            fill((me + j) % PLANE)
            spread(j, k, kind).start()
            return carry

        lax.fori_loop(1, PLANE, body, 0)
        fill(me)
        pltpu.make_async_copy(
            dsp.at[k, kind, me], out_ref.at[:, k // 2, k % 2, me, h + kind * (1 - 2 * h)],
            p_r).start()

    def finish(k):
        def gone(copy, pieces):
            for m in pieces:
                if some[m]:
                    copy(m, k).wait_send()

        @pl.when(outer)
        def _():
            gone(send_a, range(9))
            gone(send_x, FAR)

        @pl.when(inner)
        def _():
            gone(send_b, ONWARD)
            gone(send_c, HOME)
            send_u(k).wait_send()

    def step(t, carry):
        k = t - 1

        def ahead(*runs):
            @pl.when(t < CHUNKS)
            def _():
                for run, *args in runs:
                    run(*args)

        def behind(*runs):
            @pl.when(t >= 1)
            def _():
                for run, *args in runs:
                    run(*args)

        def from_far(*pieces):
            for m in pieces:
                if some[m]:
                    send_x(m, k).wait_recv()
            xs[...] = xf[k]
            dispatch(k, 1)

        @pl.when(outer)
        def _():
            @pl.when(t + 1 < CHUNKS)
            def _():
                for m in range(8):
                    if some[m]:
                        send_a(m, t + 1).start()

            if some[8]:
                @pl.when(t < CHUNKS)
                def _():
                    send_a(8, t).start()

            def back(m):
                if not some[m]:
                    return
                send_c(m, t).wait_recv()
                n, low, high = pieces_of[m]
                c[n, t, pl.ds(low, high - low)] = total(5 + n, m, t, (c, n))
                send_x(m, t).start()

            def last(m):
                send_c(m, k).wait_recv()
                _, low, high = pieces_of[m]
                sf[k, pl.ds(low, high - low)] = total(7, m, k, (c, 2))

            behind((from_far, 1, 2), (last, 5), (last, 6), (dispatch, k, 0))
            ahead((back, 0), (back, 1), (back, 2))

        @pl.when(inner)
        def _():
            def forward(m):
                if not some[m]:
                    return
                send_a(m, t).wait_recv()
                n, low, high = pieces_of[m]
                a[n, t, pl.ds(low, high - low)] = total(n, m, t, (a, n))
                send_b(m, t).start()

            def back(m):
                if not some[m]:
                    return
                send_b(m, t).wait_recv()
                n, low, high = pieces_of[m]
                b[n, t, pl.ds(low, high - low)] = total(5 + n, m, t, (b, n))
                send_c(m, t).start()

            def last(m, across, q):
                if not some[m]:
                    return
                send_a(m, q).wait_recv()
                send_b(across, q).wait_recv()
                _, low, high = pieces_of[m]
                sf[q, pl.ds(low, high - low)] = total(4, m, q, (a, 4), (b, 3))

            def both():
                last(4, 3, t)
                send_u(t).start()

            def arrive():
                send_u(k).wait_recv()
                from_far(0)

            behind((arrive,))
            ahead((forward, 0), (forward, 1), (forward, 2), (back, 0), (forward, 3), (back, 1),
                  (back, 2), (forward, 5), (both,), (forward, 6), (forward, 7), (back, 5))
            behind((last, 8, 7, k))
            ahead((back, 6))
            behind((dispatch, k, 0))

        @pl.when(t >= 2)
        def _():
            finish(t - 2)

        return carry

    lax.fori_loop(0, CHUNKS + 1, step, 0)
    finish(CHUNKS - 1)

    leaving = dsp.at[:, :, pl.ds(0, PLANE - 1)]
    pltpu.make_async_copy(leaving, leaving, p_s).wait()
    pltpu.make_async_copy(out_ref, out_ref, p_r).wait()


def run_exchange(ident, sure, tab, grads):
    full = PER - sure
    rows, cols = grads.shape[1:]
    dma = pltpu.SemaphoreType.DMA
    vmem = lambda *shape: pltpu.VMEM(shape, jnp.bfloat16)
    return pl.pallas_call(
        functools.partial(exchange, sure),
        out_shape=jax.ShapeDtypeStruct((CAP, 2, 2, PLANE, HALVES, TR, TC), jnp.bfloat16),
        in_specs=[
            pl.BlockSpec(memory_space=pltpu.SMEM),
            pl.BlockSpec(memory_space=pl.ANY),
        ],
        out_specs=pl.BlockSpec(memory_space=pl.ANY),
        scratch_shapes=[
            *[vmem(PER, rows, cols) for _ in range(4)],
            vmem(8, CHUNKS, full, TR, TC),
            vmem(5, CHUNKS, full, TR, TC),
            vmem(4, CHUNKS, full, TR, TC),
            vmem(3, CHUNKS, full, TR, TC),
            vmem(CHUNKS, full, TR, TC),
            vmem(full, TR, TC),
            vmem(CHUNKS, full, TR, TC),
            vmem(CHUNKS, HALVES, PLANE, CAP, TR, TC),
            dma((4,)),
            dma((9, CHUNKS)), dma((9, CHUNKS)),
            dma((9, CHUNKS)), dma((9, CHUNKS)),
            dma((9, CHUNKS)), dma((9, CHUNKS)),
            dma((3, CHUNKS)), dma((3, CHUNKS)),
            dma((CHUNKS,)), dma((CHUNKS,)),
            pltpu.SemaphoreType.DMA, pltpu.SemaphoreType.DMA,
        ],
        compiler_params=pltpu.CompilerParams(
            collective_id=ident, has_side_effects=True, vmem_limit_bytes=48 * 2**20),
        name=f"exchange{sure}",
    )(tab, grads)


def newton(scale_out, tab_ref, x_ref, out_ref, y_ref, sems):
    cols = 2 * TC
    half_rows = PLANE * HALVES * TR
    f32 = jnp.float32
    row = lax.broadcasted_iota(jnp.int32, (cols, cols), 0)
    col = lax.broadcasted_iota(jnp.int32, (cols, cols), 1)
    eye = (row == col).astype(f32)
    live = tab_ref[10, lax.axis_index("fsdp")]

    def dot(p, q):
        return jnp.dot(p.astype(jnp.bfloat16), q.astype(jnp.bfloat16), preferred_element_type=f32)

    def half(s, r):
        return jnp.concatenate(
            [x_ref[s, r, c].reshape(half_rows, TC) for c in range(2)], axis=1)

    grams, maps, scales = [], [], []
    for s in range(CAP):
        gram = jnp.zeros((cols, cols), f32)
        for r in range(2):
            part = half(s, r)
            gram += lax.dot_general(part, part, (((0,), (0,)), ((), ())), preferred_element_type=f32)
        norm = jnp.sqrt(jnp.sum(gram * eye, keepdims=True))
        inv = 1.0 / (norm + 1e-07)
        grams.append(gram * inv * inv)
        scales.append(jnp.where(s < live, inv * scale_out, 0.0))
        maps.append(None)
    for it in range(3):
        for s in range(CAP):
            gram = grams[s]
            poly = 3.4445 * eye - 4.775 * gram + 2.0315 * dot(gram, gram)
            maps[s] = poly if maps[s] is None else dot(maps[s], poly)
            if it < 2:
                grams[s] = dot(poly, dot(gram, poly))
    for s in range(CAP):
        last = (maps[s] * scales[s]).astype(jnp.bfloat16)
        for r in range(2):
            y = jnp.dot(half(s, r), last, preferred_element_type=f32)
            y = y.astype(jnp.bfloat16).reshape(PLANE, HALVES, TR, cols)
            for hh in range(HALVES):
                y_ref[s, r, hh] = y[:, hh]
            pltpu.make_async_copy(y_ref.at[s, r], out_ref.at[s, :, :, r], sems.at[s, r]).start()
    for s in range(CAP):
        for r in range(2):
            pltpu.make_async_copy(y_ref.at[s, r], out_ref.at[s, :, :, r], sems.at[s, r]).wait()


def tables(owner_ref, tab_ref, tier_ref):
    f32 = jnp.float32
    g = lax.axis_index("dp")
    h = lax.axis_index("fsdp") // PLANE
    groups = owner_ref.shape[1] // PER
    owner = jnp.concatenate([owner_ref[:, b * PER:(b + 1) * PER] for b in range(groups)], axis=0)
    sub = lax.broadcasted_iota(jnp.int32, (PER, PER), 0)
    lane = lax.broadcasted_iota(jnp.int32, (PER, PER), 1)
    before = (sub < lane).astype(f32)
    index = lax.broadcasted_iota(jnp.int32, (groups, PER), 1).astype(f32)
    far = (owner >= PLANE).astype(f32)
    ones_before = jnp.dot(far, before, preferred_element_type=f32)
    near_count = PER - jnp.sum(far, axis=1, keepdims=True)
    order = jnp.where(far > 0, near_count + ones_before, index - ones_before)
    fewest = jnp.min(jnp.minimum(near_count, PER - near_count), axis=0, keepdims=True)
    sure, tier = jnp.full((1, 1), float(SURES[-1]), f32), jnp.full((1, 1), float(len(SURES)), f32)
    for number, count in reversed(tuple(enumerate(SURES))):
        sure = jnp.where(fewest >= count, float(count), sure)
        tier = jnp.where(fewest >= count, float(number), tier)
    key = jnp.where(order >= PER - sure, order - (PER - sure), jnp.where(order >= sure, order, -1.0))
    subf = sub.astype(f32)
    weight = lax.broadcasted_iota(jnp.int32, (8, PER), 1).astype(f32)

    def rowdot(left, hot):
        out = lax.dot_general(left, hot, (((1,), (1,)), ((), ())), preferred_element_type=f32)
        return out[0:1].astype(jnp.int32)

    tab_ref[...] = jnp.zeros_like(tab_ref)
    for blk in range(groups):
        for half, keys in enumerate((order, key)):
            hot = (keys[blk:blk + 1] == subf).astype(f32)
            tab_ref[2 * blk + half:2 * blk + half + 1, 0:PER] = rowdot(weight, hot)
    mine = lax.broadcasted_iota(jnp.int32, (groups, PER), 0) == g
    own = jnp.sum(jnp.where(mine, owner, 0), axis=0, keepdims=True)
    place = jnp.sum(jnp.where(mine, jnp.where(h == 0, order, key), 0.0), axis=0, keepdims=True)
    has = (own == sub).astype(f32)
    slot = jnp.sum(has * jnp.dot(has, before, preferred_element_type=f32), axis=0, keepdims=True)
    place = jnp.broadcast_to(place, (8, PER))
    for s in range(CAP):
        tab_ref[8 + s:9 + s, 0:PER] = rowdot(place, has * (slot == s).astype(f32))
    tab_ref[10:11, 0:PER] = rowdot(jnp.ones((8, PER), f32), has)
    tier_ref[...] = tier.astype(jnp.int32)


def per_device(grads, owner):
    local = grads[0]
    mats, rows, cols = local.shape
    scale_out = 0.2 * math.sqrt(max(rows * PLANE * HALVES, cols))
    tab, tier = pl.pallas_call(
        tables,
        out_shape=(jax.ShapeDtypeStruct((16, 128), jnp.int32), jax.ShapeDtypeStruct((1, 1), jnp.int32)),
        in_specs=[pl.BlockSpec(memory_space=pltpu.VMEM)],
        out_specs=(pl.BlockSpec(memory_space=pltpu.VMEM), pl.BlockSpec(memory_space=pltpu.VMEM)),
        name="tables",
    )(owner.reshape(1, mats))
    ways = [functools.partial(run_exchange, 1 + n, sure) for n, sure in enumerate(SURES)]
    gathered = lax.switch(tier[0, 0], ways, tab, local)
    owned = pl.pallas_call(
        functools.partial(newton, scale_out),
        out_shape=jax.ShapeDtypeStruct((CAP, HALVES, PLANE, 2, TR, cols), jnp.bfloat16),
        in_specs=[pl.BlockSpec(memory_space=pltpu.SMEM), pl.BlockSpec(memory_space=pltpu.VMEM)],
        out_specs=pl.BlockSpec(memory_space=pl.ANY),
        scratch_shapes=[
            pltpu.VMEM((CAP, 2, HALVES, PLANE, TR, cols), jnp.bfloat16),
            pltpu.SemaphoreType.DMA((CAP, 2)),
        ],
        compiler_params=pltpu.CompilerParams(vmem_limit_bytes=48 * 2**20),
        name="newton",
    )(tab, gathered)
    return owned.reshape(1, 1, CAP, HALVES * PLANE * rows, cols)


def solution(mesh):
    placed = (P("dp", None, "fsdp", None), P())
    return jax.shard_map(
        per_device,
        mesh=mesh,
        in_specs=placed,
        out_specs=P("dp", "fsdp", None, None, None),
        check_vma=False,
    )
```
